32 devices in a mesh: wide: 8 (over z, y), narrow: 4 (over x, core).
Axes of the slice: x: 2, y: 2, z: 4, core: 2. Of those that a mesh axis runs over, the one named last changes fastest.
Arguments:
- factors: bfloat16 [15, 7168, 1920], P(None, ('wide', 'narrow')), may hold values from -0.625 to 0.625
- t2_window: bfloat16 [16, 15, 15], replicated, may hold values from -0.3984375 to 0.3984375
- residual_in: bfloat16 [232, 16, 16384], P('wide', 'narrow'), may hold values from -6 to 6
- tile_mask: int32 [225], replicated, may hold values from 0 to 1, as said below
- owner_slot: int32 [225], replicated, may hold values from 0 to 15, as said below
- home_slot: int32 [225], replicated, may hold values from 0 to 231, as said below
Outputs:
- residual_out: bfloat16 [232, 16, 16384], P('wide', 'narrow')
- ladder_norms: float32 [16, 16], P('wide', 'narrow')
The draws below stay inside these ranges and needn't reach their ends.
Inputs may be any that keep to these rules, and one draw needn't show every extreme that they name: `tile_mask`: exactly 16 tiles are filled. `owner_slot`: the filled tiles take the owner slots 0 to 15, one each; slot o belongs to wide index o // 2; the filled tiles of one wide index have different home wide indices. Entries of tiles that are not filled mean nothing. `home_slot`: all different; home slot s lies on wide index s // 29.
All inputs are finite; a program needn't handle non-finite values.
Results may differ from the reference program's by a relative error of at most 0.0045.
Values may be sent and summed in bfloat16 or wider, within the bound.
No kernel may reach another device: no remote copies, remote signals or barrier semaphores. Data moves between devices by JAX's collectives and lax.ppermute only.
A program may use at most 192 MiB of HBM per device.

```python
import jax
import jax.numpy as jnp
from jax import lax

VT = 128
NAUX = 7168
W = 15
SLOTS = 2
NC = 15
NT = 225
WVT = 1920
NP = 16
FILLED = 16
HOME_DEV = 29
HOMES = 232
N_WIDE = 8


def plan_tiles(key):
    key_home, key_fill, key_owner, key_spare = jax.random.split(key, 4)
    home_raw = jax.random.permutation(key_home, HOMES)[:NT].astype(jnp.int32)
    home_slot = jnp.where(home_raw == jnp.max(home_raw), HOMES - 1, home_raw)
    home_slot = jnp.where(home_raw == jnp.min(home_raw), 0, home_slot)
    usable = home_slot % HOME_DEV < min(HOME_DEV, N_WIDE)
    fill_rank = jax.random.permutation(key_fill, NT).astype(jnp.int32)
    fill_order = jnp.argsort(jnp.where(usable, 0, NT) + fill_rank)
    tile_mask = jnp.zeros((NT,), jnp.int32).at[fill_order[:FILLED]].set(1)
    tile_ids = jnp.arange(NT, dtype=jnp.int32)
    sort_key = jnp.where(tile_mask == 1, home_slot // HOME_DEV * NT + tile_ids, HOMES * NT + tile_ids)
    by_home = jnp.argsort(sort_key)
    position = jnp.zeros((NT,), jnp.int32).at[by_home].set(tile_ids)
    owner_order = jax.random.permutation(key_owner, N_WIDE).astype(jnp.int32)
    assigned = owner_order[position % N_WIDE] * SLOTS + position // N_WIDE
    spare_slot = jax.random.randint(key_spare, (NT,), 0, FILLED, dtype=jnp.int32)
    owner_slot = jnp.where(tile_mask == 1, assigned, spare_slot)
    return (tile_mask, owner_slot, home_slot)


def draw_tile_mask(key, part):
    shared = plan_tiles(key)
    return shared[0]


def draw_owner_slot(key, part):
    shared = plan_tiles(key)
    return shared[1]


def draw_home_slot(key, part):
    shared = plan_tiles(key)
    return shared[2]


def block_levels(stream_key, dims, cuts, smallest, largest):
    gain, own = 1.0, jax.random.fold_in(stream_key, 6)
    for dim, blocks in cuts:
        steps = jnp.exp(jax.random.uniform(jax.random.fold_in(own, dim), (blocks,), jnp.float32, smallest / len(cuts), largest / len(cuts)))
        gain = gain * jnp.repeat(steps, dims[dim] // blocks).reshape([-1 if axis == dim else 1 for axis in range(len(dims))])
    return gain


def bell_draw(key, shape, width, limit, pieces=(), held_as=jnp.bfloat16):
    array = width * jax.random.normal(key, shape, jnp.float32)
    if pieces:
        array = array * block_levels(key, shape, pieces, -0.22, 0.18)
    return jnp.clip(array, -limit, limit).astype(held_as)


def setup_inputs(seed: int = 0) -> dict:
    key_of = jax.random.split(jax.random.key(seed), 7)
    factors = bell_draw(key_of[0], (NC, NAUX, WVT), (NAUX ** 0.5) ** -0.5, 0.625, ((1, 32),))
    t2_window = bell_draw(key_of[1], (NP, W, W), (W ** -1), 0.3984375)
    residual_in = bell_draw(key_of[2], (HOMES, NP, VT * VT), 1.0, 6.0, ((0, 8), (1, 4)))
    tile_mask = draw_tile_mask(jax.random.fold_in(key_of[6], 71), 0)
    owner_slot = draw_owner_slot(jax.random.fold_in(key_of[6], 71), 0)
    home_slot = draw_home_slot(jax.random.fold_in(key_of[6], 71), 0)
    return dict(factors=factors, t2_window=t2_window, residual_in=residual_in, tile_mask=tile_mask, owner_slot=owner_slot, home_slot=home_slot)


def tile_ladder(factors, amplitude, tile):
    clusters = factors.shape[0]
    window = amplitude.shape[1]
    tile_width = factors.shape[2] // window
    first_side = lax.dynamic_index_in_dim(factors, tile // clusters, 0, keepdims=False)
    second_side = lax.dynamic_index_in_dim(factors, tile % clusters, 0, keepdims=False)
    integral = jnp.dot(first_side.T, second_side, preferred_element_type=jnp.float32)
    summed = jnp.einsum("cadb,pcd->pab", integral.reshape(window, tile_width, window, tile_width), amplitude, precision=lax.Precision.HIGHEST)
    return summed.reshape(amplitude.shape[0], tile_width * tile_width).astype(jnp.bfloat16)


def reference(factors, t2_window, residual_in, tile_mask, owner_slot, home_slot):
    amplitude = t2_window.astype(jnp.float32)
    tile_ids = jnp.arange(NT, dtype=jnp.int32)
    is_filled = tile_mask == 1
    owner_match = is_filled[:, None] & (owner_slot[:, None] == jnp.arange(FILLED, dtype=jnp.int32)[None, :])
    tile_of_slot = jnp.sum(jnp.where(owner_match, tile_ids[:, None], 0), axis=0).astype(jnp.int32)
    ladders = lax.map(lambda tile: tile_ladder(factors, amplitude, tile), tile_of_slot)
    ladder_wide = ladders.astype(jnp.float32)
    ladder_norms = jnp.mean(ladder_wide * ladder_wide, axis=2)
    present = is_filled[:, None] & (home_slot[:, None] == jnp.arange(HOMES, dtype=jnp.int32)[None, :])
    kept_slot = jnp.any(present, axis=0)
    source_slot = jnp.sum(jnp.where(present, owner_slot[:, None], 0), axis=0).astype(jnp.int32)
    picked = jnp.take(ladders, source_slot, axis=0).astype(jnp.float32)
    combined = residual_in.astype(jnp.float32) + picked
    residual_out = jnp.where(kept_slot[:, None, None], combined, 0.0).astype(jnp.bfloat16)
    return residual_out, ladder_norms
```

```python
import functools

import jax
import jax.numpy as jnp
from jax import lax
from jax.experimental import pallas as pl
from jax.experimental.pallas import tpu as pltpu
from jax.sharding import PartitionSpec as P

SLOTS = 2
ROWS = 16
WIDTH = 128
DEPTH = 256
TOGETHER = 4
STEP = 3
LADDER_VMEM = 52 * 1024 * 1024
SMALL_VMEM = 24 * 1024 * 1024
GATHER_VMEM = 60 * 1024 * 1024
HBM = pl.BlockSpec(memory_space=pltpu.HBM)


class Layout:
    def __init__(self, owners, homes):
        sizes = dict(
            own_first=owners,
            own_second=owners,
            partner_first=owners,
            partner_second=owners,
            pick=owners,
            arrive=owners + 1,
            filled=homes,
            norm=SLOTS,
            matched=1,
            half=1,
        )
        self.size = 0
        for name, size in sizes.items():
            setattr(self, name, self.size)
            self.size += size


def plan_kernel(
    place, table, plan, tile_of, home_of, official, wide_of, spot, room, load, used, slot_tile, slot_home, good,
    *, layout, names, clusters, homes
):
    wide, half = place[0], place[1]
    owners = len(names)
    filled = owners * SLOTS
    across = owners // 2

    def each(count, step, unroll=1):
        def run(i, carry):
            step(i)
            return carry

        lax.fori_loop(0, count, run, 0, unroll=unroll)

    def list_tile(t, count):
        entry = table[t]
        tile_of[count] = t
        home_of[count] = entry
        return count + (entry & 1)

    total = table.shape[0]
    lax.fori_loop(0, total, list_tile, 0, unroll=5 if total % 5 == 0 else 1)

    def clear_wide(w):
        room[w] = SLOTS
        load[w] = 0

    def clear_used(i):
        used[i] = 0

    each(owners, clear_wide)
    each(owners * owners, clear_used, 8)

    def count_home(i):
        entry = home_of[i] // SLOTS
        official[i] = entry % filled
        home_of[i] = entry // filled
        wide_of[i] = home_of[i] // homes
        load[wide_of[i]] = load[wide_of[i]] + 1
        spot[i] = -1

    each(filled, count_home)
    good[0] = 1

    def put(i, w):
        spot[i] = w * SLOTS + SLOTS - room[w]
        room[w] = room[w] - 1

    low = lax.fori_loop(0, across, lambda h, x: x + load[h], 0)
    excess = jnp.abs(low - owners)
    begin = jnp.where(low > owners, 0, across)

    def move_one(r):
        @pl.when(r < excess)
        def _():
            def fuller(h, best):
                better = (load[begin + h] > best[1]) & (used[((begin + h) ^ across) * owners + begin + h] == 0)
                return jnp.where(better, begin + h, best[0]), jnp.where(better, load[begin + h], best[1])

            best, most = lax.fori_loop(0, across, fuller, (jnp.int32(0), jnp.int32(0)))

            @pl.when(most == 0)
            def _():
                good[0] = 0

            @pl.when(most > 0)
            def _():
                found = lax.fori_loop(
                    0, filled, lambda i, x: jnp.where((wide_of[i] == best) & (spot[i] < 0), i, x), jnp.int32(0)
                )
                put(found, best ^ across)
                used[(best ^ across) * owners + best] = 1
                load[best] = load[best] - 1

    @pl.when(excess > across)
    def _():
        good[0] = 0

    each(across, move_one)

    def put_home(i):
        @pl.when((spot[i] < 0) & (room[wide_of[i]] > 0))
        def _():
            put(i, wide_of[i])

    each(filled, put_home)

    def put_near(i):
        @pl.when(spot[i] < 0)
        def _():
            def try_near(k):
                w = wide_of[i] ^ (k + 1)

                @pl.when((spot[i] < 0) & (room[w] > 0) & (used[w * owners + wide_of[i]] == 0))
                def _():
                    put(i, w)
                    used[w * owners + wide_of[i]] = 1

            each(across - 1, try_near)

            @pl.when(spot[i] < 0)
            def _():
                good[0] = 0

    each(filled, put_near)

    @pl.when(good[0] == 0)
    def _():
        def keep_owner(i):
            spot[i] = official[i]

        each(filled, keep_owner)

    def clear_filled(i):
        plan[layout.filled + i] = 0

    each(homes, clear_filled)

    def enter(i):
        slot_tile[spot[i]] = tile_of[i]
        slot_home[spot[i]] = home_of[i]

        @pl.when(official[i] // SLOTS == wide)
        def _():
            plan[layout.norm + official[i] % SLOTS] = ((spot[i] // SLOTS) ^ wide) * SLOTS + spot[i] % SLOTS

        @pl.when(wide_of[i] == wide)
        def _():
            plan[layout.filled + home_of[i] - wide * homes] = 1

    each(filled, enter)

    for j, name in enumerate(names):
        base = (wide ^ name) * SLOTS
        own, other = slot_tile[base + half], slot_tile[base + 1 - half]
        plan[layout.own_first + j] = own // clusters
        plan[layout.own_second + j] = own % clusters
        plan[layout.partner_first + j] = other // clusters
        plan[layout.partner_second + j] = other % clusters

    def at_home(slot, w):
        local = slot_home[slot] - w * homes
        return jnp.where((local >= 0) & (local < homes), local, -1)

    mine = wide * SLOTS
    plan[layout.arrive] = at_home(mine + half, wide)
    plan[layout.arrive + 1] = at_home(mine + 1 - half, wide)

    def meet(k):
        w = wide ^ k
        plan[layout.arrive + 1 + k] = jnp.maximum(at_home(w * SLOTS, wide), at_home(w * SLOTS + 1, wide))
        second = (at_home(mine + 1, w) >= 0).astype(jnp.int32)
        plan[layout.pick + k] = second ^ half

    def meet_later(k):
        meet(k + 1)

    plan[layout.pick] = 0
    each(owners - 1, meet_later)
    plan[layout.matched] = good[0]
    plan[layout.half] = half


def make_plan(place, tile_mask, owner_slot, home_slot, layout, names, clusters, homes):
    owners = len(names)
    filled = owners * SLOTS
    smem = pl.BlockSpec(memory_space=pltpu.SMEM)
    lists = [filled + 1] * 3 + [filled] * 2 + [owners] * 2 + [owners * owners] + [filled] * 2 + [1]
    return pl.pallas_call(
        functools.partial(plan_kernel, layout=layout, names=names, clusters=clusters, homes=homes),
        in_specs=[smem] * 2,
        out_specs=smem,
        out_shape=jax.ShapeDtypeStruct((layout.size,), jnp.int32),
        scratch_shapes=[pltpu.SMEM((size,), jnp.int32) for size in lists],
        compiler_params=pltpu.CompilerParams(vmem_limit_bytes=SMALL_VMEM),
    )(place, tile_mask + SLOTS * (owner_slot + filled * home_slot))


def turn_columns(source, target, slot, d, place):
    columns = pl.ds(pl.multiple_of(d * WIDTH, WIDTH), WIDTH)
    rows = source.shape[-2]
    view = source.at[0, 0] if len(source.shape) == 4 else source.at[0]
    target[slot, columns, place : place + rows] = view[:, columns].T


def partial_kernel(plan, *refs, layout, window, rows, is_first, is_last, waits, gathers):
    refs = list(refs)
    take = lambda count: [refs.pop(0) for _ in range(count)]
    kron_ref = take(1)[0]
    coming = [] if is_last else take(4)
    given = take(4) if is_first else take(2)
    take(waits)
    factors_ref = take(1)[0] if gathers else None
    keep_ref, send_ref = take(2)
    handed = [] if is_last else take(2)
    gathered = take(len(gathers))
    turned_first, turned_second, integral, total, sems = take(5)
    staged, load_sems, store_sems = take(3) if gathers else (None, None, None)
    turned = (turned_first, turned_second)
    step = pl.program_id(0)
    ends = pl.num_programs(0) - 1
    now = lax.rem(step, 2)
    later = 1 - now
    blocks = WIDTH // ROWS
    places = (0, DEPTH)

    loads, stores = [], []
    for group, (begin, count) in zip(gathered, gathers):
        for t in range(count):
            for side in range(2):
                n = len(loads)
                source = factors_ref.at[plan[(layout.partner_first, layout.partner_second)[side] + begin + t]]
                loads.append(pltpu.make_async_copy(source, staged.at[n], load_sems.at[n]))
                stores.append(pltpu.make_async_copy(staged.at[n], group.at[t, side], store_sems.at[n]))
    for load in loads:
        load.start()

    @pl.when(step == 0)
    def _():
        if is_first:
            blank = jnp.zeros((2, window * WIDTH, DEPTH - rows), jnp.bfloat16)
            for which in range(2):
                for half, place in enumerate(places):
                    turned[which][:, :, place + rows : place + DEPTH] = blank
                    for d in range(window):
                        turn_columns(given[2 * which + half], turned[which], 0, d, place)
        else:
            takes = [pltpu.make_async_copy(given[i], turned[i].at[0], sems.at[i]) for i in range(2)]
            for copy in takes:
                copy.start()
            if not is_last:
                blank = jnp.zeros((window * WIDTH, DEPTH - rows), jnp.bfloat16)
                for which in range(2):
                    for place in places:
                        turned[which][1, :, place + rows : place + DEPTH] = blank
            for copy in takes:
                copy.wait()

    def hand_on(i):
        return pltpu.make_async_copy(turned[i].at[later], handed[i], sems.at[2 + i])

    def one_block(block, carry):
        pieces = []
        for part in range(TOGETHER):
            start = pl.multiple_of((block * TOGETHER + part) * ROWS, ROWS)
            pieces += [turned_first[now, pl.ds(c * WIDTH + start, ROWS), :] for c in range(window)]
            pieces.append(jnp.zeros((DEPTH - window * ROWS, 2 * DEPTH), jnp.bfloat16))
        right = jnp.concatenate(pieces, axis=0)
        product = lax.dot_general(
            turned_second[now], right, (((1,), (1,)), ((), ())), preferred_element_type=jnp.float32
        )
        if not is_last:
            rounds = blocks // TOGETHER
            for d in range(pl.cdiv(window, rounds)):
                for half in range(2):
                    turn_columns(
                        coming[half], turned_first, later, jnp.minimum(block + d * rounds, window - 1), places[half]
                    )
        for part in range(TOGETHER):
            integral[block * TOGETHER + part] = product[:, part * DEPTH : (part + 1) * DEPTH].astype(jnp.bfloat16)
        return carry

    lax.fori_loop(0, blocks // TOGETHER, one_block, 0)
    for load, store in zip(loads, stores):
        load.wait()
        store.start()
    if not is_last:

        @pl.when(step == ends)
        def _():
            hand_on(0).start()

    for d in range(0, window, STEP):
        parts = range(d, min(d + STEP, window))
        left = jnp.concatenate(
            [integral[:, e * WIDTH : (e + 1) * WIDTH, :].reshape(blocks * WIDTH, DEPTH) for e in parts], axis=1
        )
        product = jnp.dot(
            left, kron_ref[d * DEPTH : (d + len(parts)) * DEPTH, :], preferred_element_type=jnp.float32
        )
        if not is_last:
            for e in parts:
                for half in range(2):
                    turn_columns(coming[2 + half], turned_second, later, e, places[half])
        if d == 0:
            total[...] = product
        else:
            total[...] += product

    for block in range(blocks):
        lines = slice(block * WIDTH, (block + 1) * WIDTH)
        keep_ref[0, block] = total[lines, :WIDTH].astype(jnp.bfloat16)
        send_ref[0, block] = total[lines, WIDTH:].astype(jnp.bfloat16)

    if not is_last:

        @pl.when(step == ends)
        def _():
            hand_on(1).start()
            hand_on(0).wait()
            hand_on(1).wait()

    for store in stores:
        store.wait()


def partial_ladders(plan, layout, begin, tiles, factors, partner, kron, given, window, waits, gathers, is_last):
    rows, columns = factors.shape[1:]
    blocks = WIDTH // ROWS
    side = (1, rows, columns)
    once = pl.Buffered(1)
    turned_shape = (columns, 2 * DEPTH)
    is_first = given is None
    first, second = layout.own_first + begin, layout.own_second + begin
    operands = [kron]
    in_specs = [pl.BlockSpec(kron.shape, lambda j, p: (0, 0), pipeline_mode=once)]
    skip = 1 if is_first else 0
    if not is_last:
        operands += [factors, partner, factors, partner]
        in_specs += [
            pl.BlockSpec(side, lambda j, p: (p[first + j + 1], 0, 0)),
            pl.BlockSpec((1,) + side, lambda j, p: (j + skip, 0, 0, 0)),
            pl.BlockSpec(side, lambda j, p: (p[second + j + 1], 0, 0)),
            pl.BlockSpec((1,) + side, lambda j, p: (j + skip, 1, 0, 0)),
        ]
    if is_first:
        operands += [factors, partner, factors, partner]
        in_specs += [
            pl.BlockSpec(side, lambda j, p: (p[first], 0, 0), pipeline_mode=once),
            pl.BlockSpec((1,) + side, lambda j, p: (0, 0, 0, 0), pipeline_mode=once),
            pl.BlockSpec(side, lambda j, p: (p[second], 0, 0), pipeline_mode=once),
            pl.BlockSpec((1,) + side, lambda j, p: (0, 1, 0, 0), pipeline_mode=once),
        ]
    else:
        operands += list(given)
        in_specs += [HBM] * 2
    operands += list(waits)
    in_specs += [HBM] * len(waits)
    if gathers:
        operands.append(factors)
        in_specs.append(HBM)
    part_spec = pl.BlockSpec((1, blocks, WIDTH, WIDTH), lambda j, p: (j, 0, 0, 0))
    part = jax.ShapeDtypeStruct((tiles, blocks, WIDTH, WIDTH), jnp.bfloat16)
    out_specs, out_shape = [part_spec, part_spec], [part, part]
    if not is_last:
        out_specs += [HBM] * 2
        out_shape += [jax.ShapeDtypeStruct(turned_shape, jnp.bfloat16)] * 2
    out_specs += [HBM] * len(gathers)
    out_shape += [jax.ShapeDtypeStruct((count, 2, rows, columns), jnp.bfloat16) for _, count in gathers]
    scratch_shapes = [
        pltpu.VMEM((2,) + turned_shape, jnp.bfloat16),
        pltpu.VMEM((2,) + turned_shape, jnp.bfloat16),
        pltpu.VMEM((blocks, columns, DEPTH), jnp.bfloat16),
        pltpu.VMEM((blocks * WIDTH, kron.shape[1]), jnp.float32),
        pltpu.SemaphoreType.DMA((4,)),
    ]
    if gathers:
        sides = 2 * sum(count for _, count in gathers)
        scratch_shapes += [
            pltpu.VMEM((sides, rows, columns), jnp.bfloat16),
            pltpu.SemaphoreType.DMA((sides,)),
            pltpu.SemaphoreType.DMA((sides,)),
        ]
    flops = tiles * 6 * columns * DEPTH * blocks * DEPTH
    return pl.pallas_call(
        functools.partial(
            partial_kernel,
            layout=layout,
            window=window,
            rows=rows,
            is_first=is_first,
            is_last=is_last,
            waits=len(waits),
            gathers=gathers,
        ),
        grid_spec=pltpu.PrefetchScalarGridSpec(
            num_scalar_prefetch=1,
            grid=(tiles,),
            in_specs=in_specs,
            out_specs=out_specs,
            scratch_shapes=scratch_shapes,
        ),
        out_shape=out_shape,
        compiler_params=pltpu.CompilerParams(vmem_limit_bytes=LADDER_VMEM),
        cost_estimate=pl.CostEstimate(
            flops=flops, bytes_accessed=tiles * 4 * rows * columns * 2 + kron.size * 2, transcendentals=0
        ),
    )(plan, *operands)


def gather_kernel(plan, factors_ref, out_ref, staged, load_sems, store_sems, *, layout, begin):
    loads, stores = [], []
    for t in range(out_ref.shape[0]):
        for side, start in enumerate((layout.partner_first, layout.partner_second)):
            n = len(loads)
            source = factors_ref.at[plan[start + begin + t]]
            loads.append(pltpu.make_async_copy(source, staged.at[n], load_sems.at[n]))
            stores.append(pltpu.make_async_copy(staged.at[n], out_ref.at[t, side], store_sems.at[n]))
    for load in loads:
        load.start()
    for load, store in zip(loads, stores):
        load.wait()
        store.start()
    for store in stores:
        store.wait()


def gather(plan, layout, factors, begin, count):
    rows, columns = factors.shape[1:]
    return pl.pallas_call(
        functools.partial(gather_kernel, layout=layout, begin=begin),
        grid_spec=pltpu.PrefetchScalarGridSpec(
            num_scalar_prefetch=1,
            grid=(1,),
            in_specs=[HBM],
            out_specs=HBM,
            scratch_shapes=[
                pltpu.VMEM((2 * count, rows, columns), factors.dtype),
                pltpu.SemaphoreType.DMA((2 * count,)),
                pltpu.SemaphoreType.DMA((2 * count,)),
            ],
        ),
        out_shape=jax.ShapeDtypeStruct((count, 2, rows, columns), factors.dtype),
        compiler_params=pltpu.CompilerParams(vmem_limit_bytes=GATHER_VMEM),
    )(plan, factors)


def combine_kernel(*refs, counts):
    ins, outs = refs[: sum(counts)], refs[sum(counts) + 1 :]
    begin = 0
    for count, out in zip(counts, outs):
        for block in range(out.shape[1]):
            value = ins[begin][0, block].astype(jnp.float32)
            for ref in ins[begin + 1 : begin + count]:
                value = value + ref[0, block].astype(jnp.float32)
            out[0, block] = value.astype(out.dtype)
        begin += count


def combine(groups, after):
    def at(place, shape):
        return pl.BlockSpec((1,) + shape[1:], lambda i: (place, 0, 0, 0))

    shape = groups[0][0][0].shape
    return pl.pallas_call(
        functools.partial(combine_kernel, counts=tuple(len(group) for group in groups)),
        grid=(1,),
        in_specs=[at(place, array.shape) for group in groups for array, place in group] + [HBM],
        out_specs=[at(0, shape)] * len(groups),
        out_shape=[jax.ShapeDtypeStruct((1,) + shape[1:], jnp.bfloat16)] * len(groups),
        compiler_params=pltpu.CompilerParams(vmem_limit_bytes=SMALL_VMEM),
    )(*[array for group in groups for array, _ in group], after)


def prepare_kernel(plan, residual_ref, out_ref, token_ref, held_ref, blank, put_sems, load_sems, *, layout):
    blank[...] = jnp.zeros_like(blank)
    token_ref[...] = jnp.zeros_like(token_ref)

    def put(i):
        return pltpu.make_async_copy(blank, out_ref.at[i], put_sems.at[i])

    def load(t):
        return pltpu.make_async_copy(residual_ref.at[plan[layout.arrive + t]], held_ref.at[t], load_sems.at[t])

    for i in range(out_ref.shape[0]):

        @pl.when(plan[layout.filled + i] == 0)
        def _():
            put(i).start()

    for t in range(held_ref.shape[0]):

        @pl.when(plan[layout.arrive + t] >= 0)
        def _():
            load(t).start()

    for i in range(out_ref.shape[0]):

        @pl.when(plan[layout.filled + i] == 0)
        def _():
            put(i).wait()

    for t in range(held_ref.shape[0]):

        @pl.when(plan[layout.arrive + t] >= 0)
        def _():
            load(t).wait()


def prepare(plan, layout, residual, tiles):
    grid_spec = pltpu.PrefetchScalarGridSpec(
        num_scalar_prefetch=1,
        grid=(1,),
        in_specs=[HBM],
        out_specs=[
            HBM,
            pl.BlockSpec((8, WIDTH), lambda i, p: (0, 0)),
            pl.BlockSpec((tiles,) + residual.shape[1:], lambda i, p: (0, 0, 0), pipeline_mode=pl.Buffered(1)),
        ],
        scratch_shapes=[
            pltpu.VMEM(residual.shape[1:], residual.dtype),
            pltpu.SemaphoreType.DMA((residual.shape[0],)),
            pltpu.SemaphoreType.DMA((tiles,)),
        ],
    )
    return pl.pallas_call(
        functools.partial(prepare_kernel, layout=layout),
        grid_spec=grid_spec,
        out_shape=[
            jax.ShapeDtypeStruct(residual.shape, residual.dtype),
            jax.ShapeDtypeStruct((8, WIDTH), jnp.float32),
            jax.ShapeDtypeStruct((tiles,) + residual.shape[1:], residual.dtype),
        ],
        compiler_params=pltpu.CompilerParams(vmem_limit_bytes=GATHER_VMEM),
    )(plan, residual)


def finish_kernel(plan, *refs, layout):
    parts, (keep_ref, send_ref, turned) = refs[:-3], refs[-3:]
    pairs = keep_ref.shape[0]
    half = plan[layout.half]
    mine = half * pairs * ROWS
    other = (1 - half) * pairs * ROWS
    for block in range(WIDTH // ROWS):
        value = parts[0][0, block].astype(jnp.float32)
        for part in parts[1:]:
            value = value + part[0, block].astype(jnp.float32)
        turned[block] = value.T
        for row in range(ROWS):
            lanes = slice((block * ROWS + row) * WIDTH, (block * ROWS + row + 1) * WIDTH)
            for start, ref in ((mine, keep_ref), (other, send_ref)):
                piece = turned[block, pl.ds(start + row, pairs, stride=ROWS), :]
                ref[:, lanes] = piece.astype(jnp.bfloat16)


def finish(plan, layout, parts, pairs):
    out = jax.ShapeDtypeStruct((pairs, WIDTH * WIDTH), jnp.bfloat16)
    return pl.pallas_call(
        functools.partial(finish_kernel, layout=layout),
        grid_spec=pltpu.PrefetchScalarGridSpec(
            num_scalar_prefetch=1,
            grid=(1,),
            in_specs=[pl.BlockSpec(part.shape, lambda i, h: (0, 0, 0, 0)) for part in parts],
            out_specs=[pl.BlockSpec(out.shape, lambda i, h: (0, 0))] * 2,
            scratch_shapes=[pltpu.VMEM((WIDTH // ROWS, WIDTH, WIDTH), jnp.float32)],
        ),
        out_shape=[out, out],
        compiler_params=pltpu.CompilerParams(vmem_limit_bytes=SMALL_VMEM),
    )(plan, *parts)


def pick_kernel(plan, own_ref, other_ref, *slot_refs, layout):
    for k, slot_ref in enumerate(slot_refs):

        @pl.when(plan[layout.pick + 1 + k] == 0)
        def _():
            slot_ref[...] = own_ref[...]

        @pl.when(plan[layout.pick + 1 + k] != 0)
        def _():
            slot_ref[...] = other_ref[...]


def pick(plan, layout, own, other, slots):
    whole = pl.BlockSpec(own.shape, lambda i, p: (0, 0))
    return pl.pallas_call(
        functools.partial(pick_kernel, layout=layout),
        grid_spec=pltpu.PrefetchScalarGridSpec(
            num_scalar_prefetch=1,
            grid=(1,),
            in_specs=[whole, whole],
            out_specs=[whole] * slots,
        ),
        out_shape=[jax.ShapeDtypeStruct(own.shape, own.dtype)] * slots,
        compiler_params=pltpu.CompilerParams(vmem_limit_bytes=SMALL_VMEM),
    )(plan, own, other)


def squares_kernel(plan, own_ref, other_ref, after_ref, mean_ref, *, layout):
    pairs, columns = own_ref.shape
    half = plan[layout.half]
    lane = lax.broadcasted_iota(jnp.int32, (pairs, WIDTH), 1)
    means = jnp.zeros((pairs, WIDTH), jnp.float32)
    for i, ref in enumerate((own_ref, other_ref)):
        squares = jnp.zeros((pairs, WIDTH), jnp.float32)
        for a in range(columns // WIDTH):
            squares = squares + jnp.square(ref[:, a * WIDTH : (a + 1) * WIDTH].astype(jnp.float32))
        mean = jnp.sum(squares, axis=1, keepdims=True) / columns
        means = jnp.where(lane == jnp.where(half == 0, i, 1 - i), mean, means)
    mean_ref[...] = means


def mean_squares(plan, layout, own, other, after):
    whole = pl.BlockSpec(own.shape, lambda i, p: (0, 0))
    out = jax.ShapeDtypeStruct((own.shape[0], WIDTH), jnp.float32)
    return pl.pallas_call(
        functools.partial(squares_kernel, layout=layout),
        grid_spec=pltpu.PrefetchScalarGridSpec(
            num_scalar_prefetch=1,
            grid=(1,),
            in_specs=[whole, whole, HBM],
            out_specs=pl.BlockSpec(out.shape, lambda i, p: (0, 0)),
        ),
        out_shape=out,
        compiler_params=pltpu.CompilerParams(vmem_limit_bytes=SMALL_VMEM),
    )(plan, own, other, after)


def home_kernel(plan, cleared_ref, held_ref, *refs, layout):
    tiles = held_ref.shape[0]
    ladders, (out_ref, total, sems) = refs[:tiles], refs[tiles:]

    def store(t):
        return pltpu.make_async_copy(total.at[t], out_ref.at[plan[layout.arrive + t]], sems.at[t])

    for t in range(tiles):

        @pl.when(plan[layout.arrive + t] >= 0)
        def _():
            value = held_ref[t].astype(jnp.float32) + ladders[t][...].astype(jnp.float32)
            total[t] = value.astype(total.dtype)
            store(t).start()

    for t in range(tiles):

        @pl.when(plan[layout.arrive + t] >= 0)
        def _():
            store(t).wait()


def add_at_home(plan, layout, cleared, held, ladders):
    tiles = held.shape[0]
    grid_spec = pltpu.PrefetchScalarGridSpec(
        num_scalar_prefetch=1,
        grid=(1,),
        in_specs=[HBM, pl.BlockSpec(held.shape, lambda i, s: (0, 0, 0))]
        + [pl.BlockSpec(ladder.shape, lambda i, s: (0, 0)) for ladder in ladders],
        out_specs=HBM,
        scratch_shapes=[pltpu.VMEM(held.shape, held.dtype), pltpu.SemaphoreType.DMA((tiles,))],
    )
    return pl.pallas_call(
        functools.partial(home_kernel, layout=layout),
        grid_spec=grid_spec,
        out_shape=jax.ShapeDtypeStruct(cleared.shape, cleared.dtype),
        input_output_aliases={1: 0},
        compiler_params=pltpu.CompilerParams(vmem_limit_bytes=SMALL_VMEM),
    )(plan, cleared, held, *ladders)


def kron_factor(t2_window, flip):
    pairs, window = t2_window.shape[:2]
    padded = DEPTH // ROWS
    terms = window * padded
    by_term = jnp.pad(t2_window, ((0, 0), (0, padded - window), (0, 0))).transpose(2, 1, 0).reshape(terms, pairs)
    columns = jnp.arange(pairs * ROWS, dtype=jnp.int32)
    rows = jnp.arange(terms * ROWS, dtype=jnp.int32)
    pick_pair = (jnp.arange(pairs, dtype=jnp.int32)[:, None] == ((columns // ROWS) ^ flip)[None, :]).astype(
        jnp.bfloat16
    )
    pick_term = (rows[:, None] // ROWS == jnp.arange(terms, dtype=jnp.int32)[None, :]).astype(jnp.bfloat16)
    by_column = jnp.dot(by_term, pick_pair, preferred_element_type=jnp.float32).astype(jnp.bfloat16)
    wide = jnp.dot(pick_term, by_column, preferred_element_type=jnp.float32).astype(jnp.bfloat16)
    return jnp.where(rows[:, None] % ROWS == columns[None, :] % ROWS, wide, jnp.zeros((), jnp.bfloat16))


def exchange(value, axis, bit):
    count = lax.axis_size(axis)
    return lax.ppermute(value, axis, [(i, i ^ bit) for i in range(count)])


def sending_order(owner_count):
    names = sorted(range(owner_count), key=lambda name: (-bin(name).count("1"), -name))
    if owner_count > 4:
        high = owner_count // 2
        names.remove(high)
        names.insert(len(names) - 3, high)
    return names


def body(factors, t2_window, residual_in, tile_mask, owner_slot, home_slot):
    owner_count = lax.axis_size("wide")
    narrow_count = lax.axis_size("narrow")
    wide = lax.axis_index("wide")
    narrow = lax.axis_index("narrow")
    pairs, window = t2_window.shape[:2]
    own_pairs = pairs // narrow_count
    home_count = residual_in.shape[0]
    half = narrow % 2
    names = sending_order(owner_count)
    layout = Layout(owner_count, home_count)
    place = jnp.stack([wide, half]).astype(jnp.int32)
    plan = make_plan(place, tile_mask, owner_slot, home_slot, layout, names, factors.shape[0], home_count)

    most = max(1, owner_count // 4)
    ends = [1] + list(range(1 + most, owner_count - 1, most)) + [owner_count - 1, owner_count]
    begins = [0] + ends[:-1]
    last = len(ends) - 1
    group_ranges = [(0, 2)] + [(begin + 1, end - begin) for begin, end in zip(begins[1:-1], ends[1:-1])]

    def exchange_rows(value):
        return exchange(value, "narrow", 1)

    partner_rows = [exchange_rows(gather(plan, layout, factors, *group)) for group in group_ranges[:2]]
    kron = kron_factor(t2_window, narrow // 2 * (SLOTS * own_pairs))
    cleared, token, held = prepare(plan, layout, residual_in, owner_count + 1)
    arrived = {w: [] for w in range(owner_count)}
    summed = {}
    unsent = [w for w in names if w]
    given, parts = None, []

    def send_wide(calls):
        for i in range(calls):
            for place, w in enumerate(names[begins[i] : ends[i]]):
                summed.setdefault(w, [(parts[i][0], place), (parts[i][1], place)])
        ready = [w for w in unsent if w in summed and len(arrived[w]) == (w & -w).bit_length() - 1]
        if not ready:
            return []
        sent = combine([summed[w] + [(value, 0) for value in arrived[w]] for w in ready], parts[-1][0])
        for w, value in zip(ready, sent):
            unsent.remove(w)
            arrived[w & (w - 1)].append(exchange(value, "wide", w & -w))
        return list(sent)

    for i in range(last + 1):
        waits = send_wide(i - 1) if i else [token]
        keep, send, *rest = partial_ladders(
            plan,
            layout,
            begins[i],
            ends[i] - begins[i],
            factors,
            partner_rows[i] if i < last else None,
            kron,
            given,
            window,
            waits,
            tuple(group_ranges[2:]) if i == 0 else (),
            i == last,
        )
        given = rest[:2]
        partner_rows += [exchange_rows(group) for group in rest[2:]]
        parts.append((keep, exchange(send, "narrow", 2)))
    while unsent:
        send_wide(last + 1)

    keep, send = finish(plan, layout, list(parts[last]) + arrived[0], own_pairs)
    other = exchange(send, "narrow", 1)
    slots = pick(plan, layout, keep, other, owner_count - 1)
    near = owner_count // 2
    came = [exchange(slots[k - 1], "wide", k) for k in range(near, 0, -1)][::-1]

    def from_far(*values):
        return tuple(exchange(value, "wide", near + 1 + k) for k, value in enumerate(values))

    def from_none(*values):
        return tuple(jnp.zeros_like(value) for value in values)

    if owner_count - 1 > near:
        came += lax.cond(plan[layout.matched] == 1, from_none, from_far, *slots[near:])

    norms = mean_squares(plan, layout, keep, other, came[0])[:, :SLOTS].T
    for bit in range(owner_count.bit_length() - 1):
        norms = jnp.concatenate([norms, exchange(norms, "wide", 1 << bit)], axis=0)
    rows = plan[layout.norm : layout.norm + SLOTS]
    here = rows[:, None] == jnp.arange(norms.shape[0], dtype=jnp.int32)[None, :]
    ladder_norms = jnp.sum(jnp.where(here[:, :, None], norms[None], 0.0), axis=1)
    residual_out = add_at_home(plan, layout, cleared, held, [keep, other] + came)
    return (residual_out, ladder_norms)


def solution(mesh):
    in_specs = (P(None, ("wide", "narrow"), None), P(), P("wide", "narrow", None), P(), P(), P())
    out_specs = (P("wide", "narrow", None), P("wide", "narrow"))
    return jax.shard_map(body, mesh=mesh, in_specs=in_specs, out_specs=out_specs, check_vma=False)
```

```python
import functools

import jax
import jax.numpy as jnp
from jax import lax
from jax.experimental import pallas as pl
from jax.experimental.pallas import tpu as pltpu
from jax.sharding import PartitionSpec as P

SLOTS = 2
ROWS = 16
WIDTH = 128
DEPTH = 256
TOGETHER = 4
STEP = 3
LADDER_VMEM = 34 * 1024 * 1024
FIRST_VMEM = 46 * 1024 * 1024
SMALL_VMEM = 24 * 1024 * 1024
GATHER_VMEM = 62 * 1024 * 1024
HBM = pl.BlockSpec(memory_space=pltpu.HBM)


class Layout:
    def __init__(self, owners, homes):
        sizes = dict(
            own_first=owners,
            own_second=owners,
            partner_first=owners,
            partner_second=owners,
            pick=owners,
            arrive=owners + 1,
            filled=homes,
            norm=SLOTS,
            matched=1,
            half=1,
        )
        self.size = 0
        for name, size in sizes.items():
            setattr(self, name, self.size)
            self.size += size


def gather_copies(plan, layout, factors_ref, out_ref, begin, staged, load_sems, store_sems):
    loads, stores = [], []
    for t in range(out_ref.shape[0]):
        for start in (layout.partner_first, layout.partner_second):
            n = len(loads)
            source = factors_ref.at[plan[start + begin + t]]
            loads.append(pltpu.make_async_copy(source, staged.at[n], load_sems.at[n]))
            stores.append(pltpu.make_async_copy(staged.at[n], out_ref.at[t, n % 2], store_sems.at[n]))
    return loads, stores


def run_gather(loads, stores):
    for load in loads:
        load.start()
    for load, store in zip(loads, stores):
        load.wait()
        store.start()
    for store in stores:
        store.wait()


def over(x, divisor):
    return lax.shift_right_logical(x * (65536 // divisor + 1), 16)


def plan_kernel(
    place, table, factors_ref, plan, group_ref, tile_of, home_of, official, wide_of, spot, room, load, used, slot_tile, slot_home, good,
    staged, load_sems, store_sems, *, layout, names, clusters, homes
):
    wide, half = place[0], place[1]
    owners = len(names)
    filled = owners * SLOTS
    across = owners // 2

    def each(count, step, unroll=1):
        def run(i, carry):
            step(i)
            return carry

        lax.fori_loop(0, count, run, 0, unroll=unroll)

    def list_tile(t, count):
        entry = table[t]
        tile_of[count] = t
        home_of[count] = entry
        return count + (entry & 1)

    total = table.shape[0]
    lax.fori_loop(0, total, list_tile, 0, unroll=25 if total % 25 == 0 else 1)

    def clear_wide(w):
        room[w] = SLOTS
        load[w] = 0

    def clear_used(i):
        used[i] = 0

    each(owners, clear_wide)
    each(owners * owners, clear_used, 8)

    def count_home(i):
        entry = home_of[i] // SLOTS
        official[i] = entry % filled
        home_of[i] = entry // filled
        wide_of[i] = over(home_of[i], homes)
        load[wide_of[i]] = load[wide_of[i]] + 1
        spot[i] = -1

    each(filled, count_home)
    good[0] = 1

    def put(i, w):
        spot[i] = w * SLOTS + SLOTS - room[w]
        room[w] = room[w] - 1

    low = lax.fori_loop(0, across, lambda h, x: x + load[h], 0)
    excess = jnp.abs(low - owners)
    begin = jnp.where(low > owners, 0, across)

    def move_one(r):
        @pl.when(r < excess)
        def _():
            def fuller(h, best):
                better = (load[begin + h] > best[1]) & (used[((begin + h) ^ across) * owners + begin + h] == 0)
                return jnp.where(better, begin + h, best[0]), jnp.where(better, load[begin + h], best[1])

            best, most = lax.fori_loop(0, across, fuller, (jnp.int32(0), jnp.int32(0)))

            @pl.when(most == 0)
            def _():
                good[0] = 0

            @pl.when(most > 0)
            def _():
                found = lax.fori_loop(
                    0, filled, lambda i, x: jnp.where((wide_of[i] == best) & (spot[i] < 0), i, x), jnp.int32(0)
                )
                put(found, best ^ across)
                used[(best ^ across) * owners + best] = 1
                load[best] = load[best] - 1

    @pl.when(excess > across)
    def _():
        good[0] = 0

    each(across, move_one)

    def put_home(i):
        @pl.when((spot[i] < 0) & (room[wide_of[i]] > 0))
        def _():
            put(i, wide_of[i])

    each(filled, put_home)

    def put_near(i):
        @pl.when(spot[i] < 0)
        def _():
            def try_near(k):
                w = wide_of[i] ^ (k + 1)

                @pl.when((spot[i] < 0) & (room[w] > 0) & (used[w * owners + wide_of[i]] == 0))
                def _():
                    put(i, w)
                    used[w * owners + wide_of[i]] = 1

            each(across - 1, try_near)

            def try_move(j):
                at = spot[j]
                w, h, other = at // SLOTS, wide_of[i], wide_of[j]
                fits = (at >= 0) & (w != h) & ((w ^ h) < across) & ((w ^ other) < across) & (other != h)

                @pl.when((spot[i] < 0) & fits)
                def _():
                    def try_other(k):
                        to = w ^ (k + 1)
                        free = (room[to] > 0) & (used[w * owners + h] == 0)
                        good_place = (to == other) | (used[to * owners + other] == 0)

                        @pl.when((spot[i] < 0) & free & good_place)
                        def _():
                            used[w * owners + other] = 0
                            used[to * owners + other] = 1
                            put(j, to)
                            spot[i] = at
                            used[w * owners + h] = 1

                    each(across - 1, try_other)

            @pl.when(spot[i] < 0)
            def _():
                each(filled, try_move)

            @pl.when(spot[i] < 0)
            def _():
                good[0] = 0

    each(filled, put_near)

    @pl.when(good[0] == 0)
    def _():
        def keep_owner(i):
            spot[i] = official[i]

        each(filled, keep_owner)

    def clear_filled(i):
        plan[layout.filled + i] = 0

    each(homes, clear_filled)

    def enter(i):
        slot_tile[spot[i]] = tile_of[i]
        slot_home[spot[i]] = home_of[i]

        @pl.when(official[i] // SLOTS == wide)
        def _():
            plan[layout.norm + official[i] % SLOTS] = ((spot[i] // SLOTS) ^ wide) * SLOTS + spot[i] % SLOTS

        @pl.when(wide_of[i] == wide)
        def _():
            plan[layout.filled + home_of[i] - wide * homes] = 1

    each(filled, enter)

    for j, name in enumerate(names):
        base = (wide ^ name) * SLOTS
        other = slot_tile[base + 1 - half]
        plan[layout.partner_first + j] = over(other, clusters)
        plan[layout.partner_second + j] = other - over(other, clusters) * clusters
    loads, stores = gather_copies(plan, layout, factors_ref, group_ref, 0, staged, load_sems, store_sems)
    for load in loads:
        load.start()
    for j, name in enumerate(names):
        own = slot_tile[(wide ^ name) * SLOTS + half]
        plan[layout.own_first + j] = over(own, clusters)
        plan[layout.own_second + j] = own - over(own, clusters) * clusters

    def at_home(slot, w):
        local = slot_home[slot] - w * homes
        return jnp.where((local >= 0) & (local < homes), local, -1)

    mine = wide * SLOTS
    plan[layout.arrive] = at_home(mine + half, wide)
    plan[layout.arrive + 1] = at_home(mine + 1 - half, wide)

    def meet(k):
        w = wide ^ k
        plan[layout.arrive + 1 + k] = jnp.maximum(at_home(w * SLOTS, wide), at_home(w * SLOTS + 1, wide))
        second = (at_home(mine + 1, w) >= 0).astype(jnp.int32)
        plan[layout.pick + k] = second ^ half

    def meet_later(k):
        meet(k + 1)

    plan[layout.pick] = 0
    each(owners - 1, meet_later)
    plan[layout.matched] = good[0]
    plan[layout.half] = half
    for load, store in zip(loads, stores):
        load.wait()
        store.start()
    for store in stores:
        store.wait()


def make_plan(place, tile_mask, owner_slot, home_slot, factors, layout, names, homes, count):
    owners = len(names)
    filled = owners * SLOTS
    smem = pl.BlockSpec(memory_space=pltpu.SMEM)
    lists = [filled + 1] * 3 + [filled] * 2 + [owners] * 2 + [owners * owners] + [filled] * 2 + [1]
    clusters, rows, columns = factors.shape
    return pl.pallas_call(
        functools.partial(plan_kernel, layout=layout, names=names, clusters=clusters, homes=homes),
        in_specs=[smem, smem, HBM],
        out_specs=[smem, HBM],
        out_shape=[
            jax.ShapeDtypeStruct((layout.size,), jnp.int32),
            jax.ShapeDtypeStruct((count, 2, rows, columns), factors.dtype),
        ],
        scratch_shapes=[pltpu.SMEM((size,), jnp.int32) for size in lists]
        + [
            pltpu.VMEM((2 * count, rows, columns), factors.dtype),
            pltpu.SemaphoreType.DMA((2 * count,)),
            pltpu.SemaphoreType.DMA((2 * count,)),
        ],
        compiler_params=pltpu.CompilerParams(vmem_limit_bytes=GATHER_VMEM),
    )(place, tile_mask + SLOTS * (owner_slot + filled * home_slot), factors)


def turn_columns(source, target, slot, d, place):
    columns = pl.ds(pl.multiple_of(d * WIDTH, WIDTH), WIDTH)
    rows = source.shape[-2]
    view = source.at[0, 0] if len(source.shape) == 4 else source.at[0]
    target[slot, columns, place : place + rows] = view[:, columns].T


def partial_kernel(plan, *refs, layout, window, rows, is_first, is_last, waits, gathers):
    refs = list(refs)
    take = lambda count: [refs.pop(0) for _ in range(count)]
    kron_ref = take(1)[0]
    coming = [] if is_last else take(4)
    given = take(4) if is_first else take(2)
    take(waits)
    factors_ref = take(1)[0] if gathers else None
    keep_ref, send_ref = take(2)
    handed = [] if is_last else take(2)
    gathered = take(len(gathers))
    turned_first, turned_second, integral, total, kron, sems = take(6)
    staged, load_sems, store_sems = take(3) if gathers else (None, None, None)
    turned = (turned_first, turned_second)
    step = pl.program_id(0)
    ends = pl.num_programs(0) - 1
    now = lax.rem(step, 2)
    later = 1 - now
    blocks = WIDTH // ROWS
    places = (0, DEPTH)

    fill = pltpu.make_async_copy(kron_ref, kron, sems.at[4])
    loads, stores = [], []
    for group, (begin, count) in zip(gathered, gathers):
        for t in range(count):
            for side in range(2):
                n = len(loads)
                source = factors_ref.at[plan[(layout.partner_first, layout.partner_second)[side] + begin + t]]
                loads.append(pltpu.make_async_copy(source, staged.at[n], load_sems.at[n]))
                stores.append(pltpu.make_async_copy(staged.at[n], group.at[t, side], store_sems.at[n]))
    for load in loads:
        load.start()

    @pl.when(step == 0)
    def _():
        if is_first:
            blank = jnp.zeros((2, window * WIDTH, DEPTH - rows), jnp.bfloat16)
            for which in range(2):
                for half, place in enumerate(places):
                    turned[which][:, :, place + rows : place + DEPTH] = blank
                    for d in range(window):
                        turn_columns(given[2 * which + half], turned[which], 0, d, place)
            fill.start()
        else:
            takes = [pltpu.make_async_copy(given[i], turned[i].at[0], sems.at[i]) for i in range(2)]
            for copy in takes:
                copy.start()
            fill.start()
            if not is_last:
                blank = jnp.zeros((window * WIDTH, DEPTH - rows), jnp.bfloat16)
                for which in range(2):
                    for place in places:
                        turned[which][1, :, place + rows : place + DEPTH] = blank
            for copy in takes:
                copy.wait()

    def hand_on(i):
        return pltpu.make_async_copy(turned[i].at[later], handed[i], sems.at[2 + i])

    def one_block(block, carry):
        pieces = []
        for part in range(TOGETHER):
            start = pl.multiple_of((block * TOGETHER + part) * ROWS, ROWS)
            pieces += [turned_first[now, pl.ds(c * WIDTH + start, ROWS), :] for c in range(window)]
            pieces.append(jnp.zeros((DEPTH - window * ROWS, 2 * DEPTH), jnp.bfloat16))
        right = jnp.concatenate(pieces, axis=0)
        product = lax.dot_general(
            turned_second[now], right, (((1,), (1,)), ((), ())), preferred_element_type=jnp.float32
        )
        if not is_last:
            rounds = blocks // TOGETHER
            for d in range(pl.cdiv(window, rounds)):
                for half in range(2):
                    turn_columns(
                        coming[half], turned_first, later, jnp.minimum(block + d * rounds, window - 1), places[half]
                    )
        for part in range(TOGETHER):
            integral[block * TOGETHER + part] = product[:, part * DEPTH : (part + 1) * DEPTH].astype(jnp.bfloat16)
        return carry

    lax.fori_loop(0, blocks // TOGETHER, one_block, 0)
    for load, store in zip(loads, stores):
        load.wait()
        store.start()
    if not is_last:

        @pl.when(step == ends)
        def _():
            hand_on(0).start()

    @pl.when(step == 0)
    def _():
        fill.wait()

    for d in range(0, window, STEP):
        parts = range(d, min(d + STEP, window))
        left = jnp.concatenate(
            [integral[:, e * WIDTH : (e + 1) * WIDTH, :].reshape(blocks * WIDTH, DEPTH) for e in parts], axis=1
        )
        product = jnp.dot(
            left, kron[d * DEPTH : (d + len(parts)) * DEPTH, :], preferred_element_type=jnp.float32
        )
        if not is_last:
            for e in parts:
                for half in range(2):
                    turn_columns(coming[2 + half], turned_second, later, e, places[half])
        if d == 0:
            total[...] = product
        else:
            total[...] += product

    for block in range(blocks):
        lines = slice(block * WIDTH, (block + 1) * WIDTH)
        keep_ref[0, block] = total[lines, :WIDTH].astype(jnp.bfloat16)
        send_ref[0, block] = total[lines, WIDTH:].astype(jnp.bfloat16)

    if not is_last:

        @pl.when(step == ends)
        def _():
            hand_on(1).start()
            hand_on(0).wait()
            hand_on(1).wait()

    for store in stores:
        store.wait()


def partial_ladders(plan, layout, begin, tiles, factors, partner, kron, given, window, waits, gathers, is_last):
    rows, columns = factors.shape[1:]
    blocks = WIDTH // ROWS
    side = (1, rows, columns)
    once = pl.Buffered(1)
    turned_shape = (columns, 2 * DEPTH)
    is_first = given is None
    first, second = layout.own_first + begin, layout.own_second + begin
    operands = [kron]
    in_specs = [HBM]
    skip = 1 if is_first else 0
    if not is_last:
        operands += [factors, partner, factors, partner]
        in_specs += [
            pl.BlockSpec(side, lambda j, p: (p[first + j + 1], 0, 0)),
            pl.BlockSpec((1,) + side, lambda j, p: (j + skip, 0, 0, 0)),
            pl.BlockSpec(side, lambda j, p: (p[second + j + 1], 0, 0)),
            pl.BlockSpec((1,) + side, lambda j, p: (j + skip, 1, 0, 0)),
        ]
    if is_first:
        operands += [factors, partner, factors, partner]
        in_specs += [
            pl.BlockSpec(side, lambda j, p: (p[first], 0, 0), pipeline_mode=once),
            pl.BlockSpec((1,) + side, lambda j, p: (0, 0, 0, 0), pipeline_mode=once),
            pl.BlockSpec(side, lambda j, p: (p[second], 0, 0), pipeline_mode=once),
            pl.BlockSpec((1,) + side, lambda j, p: (0, 1, 0, 0), pipeline_mode=once),
        ]
    else:
        operands += list(given)
        in_specs += [HBM] * 2
    operands += list(waits)
    in_specs += [HBM] * len(waits)
    if gathers:
        operands.append(factors)
        in_specs.append(HBM)
    part_spec = pl.BlockSpec((1, blocks, WIDTH, WIDTH), lambda j, p: (j, 0, 0, 0))
    part = jax.ShapeDtypeStruct((tiles, blocks, WIDTH, WIDTH), jnp.bfloat16)
    out_specs, out_shape = [part_spec, part_spec], [part, part]
    if not is_last:
        out_specs += [HBM] * 2
        out_shape += [jax.ShapeDtypeStruct(turned_shape, jnp.bfloat16)] * 2
    out_specs += [HBM] * len(gathers)
    out_shape += [jax.ShapeDtypeStruct((count, 2, rows, columns), jnp.bfloat16) for _, count in gathers]
    scratch_shapes = [
        pltpu.VMEM((2,) + turned_shape, jnp.bfloat16),
        pltpu.VMEM((2,) + turned_shape, jnp.bfloat16),
        pltpu.VMEM((blocks, columns, DEPTH), jnp.bfloat16),
        pltpu.VMEM((blocks * WIDTH, kron.shape[1]), jnp.float32),
        pltpu.VMEM(kron.shape, kron.dtype),
        pltpu.SemaphoreType.DMA((5,)),
    ]
    if gathers:
        sides = 2 * sum(count for _, count in gathers)
        scratch_shapes += [
            pltpu.VMEM((sides, rows, columns), jnp.bfloat16),
            pltpu.SemaphoreType.DMA((sides,)),
            pltpu.SemaphoreType.DMA((sides,)),
        ]
    flops = tiles * 6 * columns * DEPTH * blocks * DEPTH
    return pl.pallas_call(
        functools.partial(
            partial_kernel,
            layout=layout,
            window=window,
            rows=rows,
            is_first=is_first,
            is_last=is_last,
            waits=len(waits),
            gathers=gathers,
        ),
        grid_spec=pltpu.PrefetchScalarGridSpec(
            num_scalar_prefetch=1,
            grid=(tiles,),
            in_specs=in_specs,
            out_specs=out_specs,
            scratch_shapes=scratch_shapes,
        ),
        out_shape=out_shape,
        compiler_params=pltpu.CompilerParams(vmem_limit_bytes=FIRST_VMEM if is_first else LADDER_VMEM),
        cost_estimate=pl.CostEstimate(
            flops=flops, bytes_accessed=tiles * 4 * rows * columns * 2 + kron.size * 2, transcendentals=0
        ),
    )(plan, *operands)


def gather_kernel(plan, factors_ref, out_ref, staged, load_sems, store_sems, *, layout, begin):
    run_gather(*gather_copies(plan, layout, factors_ref, out_ref, begin, staged, load_sems, store_sems))


def gather(plan, layout, factors, begin, count):
    rows, columns = factors.shape[1:]
    return pl.pallas_call(
        functools.partial(gather_kernel, layout=layout, begin=begin),
        grid_spec=pltpu.PrefetchScalarGridSpec(
            num_scalar_prefetch=1,
            grid=(1,),
            in_specs=[HBM],
            out_specs=HBM,
            scratch_shapes=[
                pltpu.VMEM((2 * count, rows, columns), factors.dtype),
                pltpu.SemaphoreType.DMA((2 * count,)),
                pltpu.SemaphoreType.DMA((2 * count,)),
            ],
        ),
        out_shape=jax.ShapeDtypeStruct((count, 2, rows, columns), factors.dtype),
        compiler_params=pltpu.CompilerParams(vmem_limit_bytes=GATHER_VMEM),
    )(plan, factors)


def combine_kernel(*refs, counts):
    ins, outs = refs[: sum(counts)], refs[sum(counts) + 1 :]
    begin = 0
    for count, out in zip(counts, outs):
        for block in range(out.shape[1]):
            value = ins[begin][0, block].astype(jnp.float32)
            for ref in ins[begin + 1 : begin + count]:
                value = value + ref[0, block].astype(jnp.float32)
            out[0, block] = value.astype(out.dtype)
        begin += count


def combine(groups, after):
    def at(place, shape):
        return pl.BlockSpec((1,) + shape[1:], lambda i: (place, 0, 0, 0))

    shape = groups[0][0][0].shape
    return pl.pallas_call(
        functools.partial(combine_kernel, counts=tuple(len(group) for group in groups)),
        grid=(1,),
        in_specs=[at(place, array.shape) for group in groups for array, place in group] + [HBM],
        out_specs=[at(0, shape)] * len(groups),
        out_shape=[jax.ShapeDtypeStruct((1,) + shape[1:], jnp.bfloat16)] * len(groups),
        compiler_params=pltpu.CompilerParams(vmem_limit_bytes=SMALL_VMEM),
    )(*[array for group in groups for array, _ in group], after)


def prepare_kernel(plan, residual_ref, after_ref, out_ref, token_ref, held_ref, blank, put_sems, load_sems, *, layout):
    blank[...] = jnp.zeros_like(blank)
    token_ref[...] = jnp.zeros_like(token_ref)

    def put(i):
        return pltpu.make_async_copy(blank, out_ref.at[i], put_sems.at[i])

    def load(t):
        return pltpu.make_async_copy(residual_ref.at[plan[layout.arrive + t]], held_ref.at[t], load_sems.at[t])

    for i in range(out_ref.shape[0]):

        @pl.when(plan[layout.filled + i] == 0)
        def _():
            put(i).start()

    for t in range(held_ref.shape[0]):

        @pl.when(plan[layout.arrive + t] >= 0)
        def _():
            load(t).start()

    for i in range(out_ref.shape[0]):

        @pl.when(plan[layout.filled + i] == 0)
        def _():
            put(i).wait()

    for t in range(held_ref.shape[0]):

        @pl.when(plan[layout.arrive + t] >= 0)
        def _():
            load(t).wait()


def prepare(plan, layout, residual, tiles, after):
    grid_spec = pltpu.PrefetchScalarGridSpec(
        num_scalar_prefetch=1,
        grid=(1,),
        in_specs=[HBM, HBM],
        out_specs=[
            HBM,
            pl.BlockSpec((8, WIDTH), lambda i, p: (0, 0)),
            pl.BlockSpec((tiles,) + residual.shape[1:], lambda i, p: (0, 0, 0), pipeline_mode=pl.Buffered(1)),
        ],
        scratch_shapes=[
            pltpu.VMEM(residual.shape[1:], residual.dtype),
            pltpu.SemaphoreType.DMA((residual.shape[0],)),
            pltpu.SemaphoreType.DMA((tiles,)),
        ],
    )
    return pl.pallas_call(
        functools.partial(prepare_kernel, layout=layout),
        grid_spec=grid_spec,
        out_shape=[
            jax.ShapeDtypeStruct(residual.shape, residual.dtype),
            jax.ShapeDtypeStruct((8, WIDTH), jnp.float32),
            jax.ShapeDtypeStruct((tiles,) + residual.shape[1:], residual.dtype),
        ],
        compiler_params=pltpu.CompilerParams(vmem_limit_bytes=LADDER_VMEM),
    )(plan, residual, after)


def mark_kernel(plan, out_ref):
    out_ref[...] = jnp.full(out_ref.shape, plan[0], out_ref.dtype)


def mark(plan):
    return pl.pallas_call(
        mark_kernel,
        grid_spec=pltpu.PrefetchScalarGridSpec(
            num_scalar_prefetch=1,
            grid=(1,),
            in_specs=[],
            out_specs=pl.BlockSpec((8, WIDTH), lambda i, p: (0, 0)),
        ),
        out_shape=jax.ShapeDtypeStruct((8, WIDTH), jnp.int32),
        compiler_params=pltpu.CompilerParams(vmem_limit_bytes=GATHER_VMEM),
    )(plan)


def finish_kernel(plan, *refs, layout):
    parts, (keep_ref, send_ref, turned) = refs[:-4], refs[-3:]
    pairs = keep_ref.shape[0]
    half = plan[layout.half]
    mine = half * pairs * ROWS
    other = (1 - half) * pairs * ROWS
    for block in range(WIDTH // ROWS):
        value = parts[0][0, block].astype(jnp.float32)
        for part in parts[1:]:
            value = value + part[0, block].astype(jnp.float32)
        turned[block] = value.T
        for row in range(ROWS):
            lanes = slice((block * ROWS + row) * WIDTH, (block * ROWS + row + 1) * WIDTH)
            for start, ref in ((mine, keep_ref), (other, send_ref)):
                piece = turned[block, pl.ds(start + row, pairs, stride=ROWS), :]
                ref[:, lanes] = piece.astype(jnp.bfloat16)


def finish(plan, layout, parts, pairs, after):
    out = jax.ShapeDtypeStruct((pairs, WIDTH * WIDTH), jnp.bfloat16)
    return pl.pallas_call(
        functools.partial(finish_kernel, layout=layout),
        grid_spec=pltpu.PrefetchScalarGridSpec(
            num_scalar_prefetch=1,
            grid=(1,),
            in_specs=[pl.BlockSpec(part.shape, lambda i, h: (0, 0, 0, 0)) for part in parts] + [HBM],
            out_specs=[pl.BlockSpec(out.shape, lambda i, h: (0, 0))] * 2,
            scratch_shapes=[pltpu.VMEM((WIDTH // ROWS, WIDTH, WIDTH), jnp.float32)],
        ),
        out_shape=[out, out],
        compiler_params=pltpu.CompilerParams(vmem_limit_bytes=SMALL_VMEM),
    )(plan, *parts, after)


def pick_kernel(plan, own_ref, other_ref, *slot_refs, layout):
    for k, slot_ref in enumerate(slot_refs):

        @pl.when(plan[layout.pick + 1 + k] == 0)
        def _():
            slot_ref[...] = own_ref[...]

        @pl.when(plan[layout.pick + 1 + k] != 0)
        def _():
            slot_ref[...] = other_ref[...]


def pick(plan, layout, own, other, slots):
    whole = pl.BlockSpec(own.shape, lambda i, p: (0, 0))
    return pl.pallas_call(
        functools.partial(pick_kernel, layout=layout),
        grid_spec=pltpu.PrefetchScalarGridSpec(
            num_scalar_prefetch=1,
            grid=(1,),
            in_specs=[whole, whole],
            out_specs=[whole] * slots,
        ),
        out_shape=[jax.ShapeDtypeStruct(own.shape, own.dtype)] * slots,
        compiler_params=pltpu.CompilerParams(vmem_limit_bytes=SMALL_VMEM),
    )(plan, own, other)


def squares_kernel(plan, own_ref, other_ref, after_ref, mean_ref, *, layout):
    pairs, columns = own_ref.shape
    half = plan[layout.half]
    lane = lax.broadcasted_iota(jnp.int32, (pairs, WIDTH), 1)
    means = jnp.zeros((pairs, WIDTH), jnp.float32)
    for i, ref in enumerate((own_ref, other_ref)):
        squares = jnp.zeros((pairs, WIDTH), jnp.float32)
        for a in range(columns // WIDTH):
            squares = squares + jnp.square(ref[:, a * WIDTH : (a + 1) * WIDTH].astype(jnp.float32))
        mean = jnp.sum(squares, axis=1, keepdims=True) / columns
        means = jnp.where(lane == jnp.where(half == 0, i, 1 - i), mean, means)
    mean_ref[...] = means


def mean_squares(plan, layout, own, other, after):
    whole = pl.BlockSpec(own.shape, lambda i, p: (0, 0))
    out = jax.ShapeDtypeStruct((own.shape[0], WIDTH), jnp.float32)
    return pl.pallas_call(
        functools.partial(squares_kernel, layout=layout),
        grid_spec=pltpu.PrefetchScalarGridSpec(
            num_scalar_prefetch=1,
            grid=(1,),
            in_specs=[whole, whole, HBM],
            out_specs=pl.BlockSpec(out.shape, lambda i, p: (0, 0)),
        ),
        out_shape=out,
        compiler_params=pltpu.CompilerParams(vmem_limit_bytes=SMALL_VMEM),
    )(plan, own, other, after)


def home_kernel(plan, cleared_ref, held_ref, *refs, layout):
    tiles = held_ref.shape[0]
    ladders, (out_ref, total, sems) = refs[:tiles], refs[tiles:]

    def store(t):
        return pltpu.make_async_copy(total.at[t], out_ref.at[plan[layout.arrive + t]], sems.at[t])

    for t in range(tiles):

        @pl.when(plan[layout.arrive + t] >= 0)
        def _():
            value = held_ref[t].astype(jnp.float32) + ladders[t][...].astype(jnp.float32)
            total[t] = value.astype(total.dtype)
            store(t).start()

    for t in range(tiles):

        @pl.when(plan[layout.arrive + t] >= 0)
        def _():
            store(t).wait()


def add_at_home(plan, layout, cleared, held, ladders):
    tiles = held.shape[0]
    grid_spec = pltpu.PrefetchScalarGridSpec(
        num_scalar_prefetch=1,
        grid=(1,),
        in_specs=[HBM, pl.BlockSpec(held.shape, lambda i, s: (0, 0, 0))]
        + [pl.BlockSpec(ladder.shape, lambda i, s: (0, 0)) for ladder in ladders],
        out_specs=HBM,
        scratch_shapes=[pltpu.VMEM(held.shape, held.dtype), pltpu.SemaphoreType.DMA((tiles,))],
    )
    return pl.pallas_call(
        functools.partial(home_kernel, layout=layout),
        grid_spec=grid_spec,
        out_shape=jax.ShapeDtypeStruct(cleared.shape, cleared.dtype),
        input_output_aliases={1: 0},
        compiler_params=pltpu.CompilerParams(vmem_limit_bytes=SMALL_VMEM),
    )(plan, cleared, held, *ladders)


def kron_factor(t2_window, flip):
    pairs, window = t2_window.shape[:2]
    padded = DEPTH // ROWS
    terms = window * padded
    by_term = jnp.pad(t2_window, ((0, 0), (0, padded - window), (0, 0))).transpose(2, 1, 0).reshape(terms, pairs)
    columns = jnp.arange(pairs * ROWS, dtype=jnp.int32)
    rows = jnp.arange(terms * ROWS, dtype=jnp.int32)
    pick_pair = (jnp.arange(pairs, dtype=jnp.int32)[:, None] == ((columns // ROWS) ^ flip)[None, :]).astype(
        jnp.bfloat16
    )
    pick_term = (rows[:, None] // ROWS == jnp.arange(terms, dtype=jnp.int32)[None, :]).astype(jnp.bfloat16)
    by_column = jnp.dot(by_term, pick_pair, preferred_element_type=jnp.float32).astype(jnp.bfloat16)
    wide = jnp.dot(pick_term, by_column, preferred_element_type=jnp.float32).astype(jnp.bfloat16)
    return jnp.where(rows[:, None] % ROWS == columns[None, :] % ROWS, wide, jnp.zeros((), jnp.bfloat16))


def exchange(value, axis, bit):
    count = lax.axis_size(axis)
    return lax.ppermute(value, axis, [(i, i ^ bit) for i in range(count)])


def sending_order(owner_count):
    names = sorted(range(owner_count), key=lambda name: (-bin(name).count("1"), -name))
    if owner_count > 4:
        high = owner_count // 2
        names.remove(high)
        names.insert(len(names) - 3, high)
    return names


def body(factors, t2_window, residual_in, tile_mask, owner_slot, home_slot):
    owner_count = lax.axis_size("wide")
    narrow_count = lax.axis_size("narrow")
    wide = lax.axis_index("wide")
    narrow = lax.axis_index("narrow")
    pairs, window = t2_window.shape[:2]
    own_pairs = pairs // narrow_count
    home_count = residual_in.shape[0]
    half = narrow % 2
    names = sending_order(owner_count)
    layout = Layout(owner_count, home_count)
    place = jnp.stack([wide, half]).astype(jnp.int32)

    most = max(1, owner_count // 4)
    ends = [1] + list(range(1 + most, owner_count - 1, most)) + [owner_count - 1, owner_count]
    begins = [0] + ends[:-1]
    last = len(ends) - 1
    plan, group = make_plan(place, tile_mask, owner_slot, home_slot, factors, layout, names, home_count, 2)
    group_ranges = [(0, 2)] + [(begin + 1, end - begin) for begin, end in zip(begins[1:-1], ends[1:-1])]

    def exchange_rows(value):
        return exchange(value, "narrow", 1)

    partner_rows = [exchange_rows(group), exchange_rows(gather(plan, layout, factors, *group_ranges[1]))]
    kron = kron_factor(t2_window, narrow // 2 * (SLOTS * own_pairs))
    token = mark(plan)
    arrived = {w: [] for w in range(owner_count)}
    summed = {}
    unsent = [w for w in names if w]
    given, parts = None, []

    def send_wide(calls):
        for i in range(calls):
            for place, w in enumerate(names[begins[i] : ends[i]]):
                summed.setdefault(w, [(parts[i][0], place), (parts[i][1], place)])
        ready = [w for w in unsent if w in summed and len(arrived[w]) == (w & -w).bit_length() - 1]
        if not ready:
            return []
        sent = combine([summed[w] + [(value, 0) for value in arrived[w]] for w in ready], parts[-1][0])
        for w, value in zip(ready, sent):
            unsent.remove(w)
            arrived[w & (w - 1)].append(exchange(value, "wide", w & -w))
        return list(sent)

    for i in range(last + 1):
        waits = send_wide(i - 1) if i else [token]
        keep, send, *rest = partial_ladders(
            plan,
            layout,
            begins[i],
            ends[i] - begins[i],
            factors,
            partner_rows[i] if i < last else None,
            kron,
            given,
            window,
            waits,
            tuple(group_ranges[2:]) if i == 0 else (),
            i == last,
        )
        given = rest[:2]
        partner_rows += [exchange_rows(group) for group in rest[2:]]
        parts.append((keep, exchange(send, "narrow", 2)))
    while unsent:
        send_wide(last + 1)

    cleared, token, held = prepare(plan, layout, residual_in, owner_count + 1, parts[last][0])
    keep, send = finish(plan, layout, list(parts[last]) + arrived[0], own_pairs, token)
    other = exchange(send, "narrow", 1)
    slots = pick(plan, layout, keep, other, owner_count - 1)
    near = owner_count // 2
    came = [exchange(slots[k - 1], "wide", k) for k in range(near, 0, -1)][::-1]

    def from_far(*values):
        return tuple(exchange(value, "wide", near + 1 + k) for k, value in enumerate(values))

    def from_none(*values):
        return tuple(jnp.zeros_like(value) for value in values)

    if owner_count - 1 > near:
        came += lax.cond(plan[layout.matched] == 1, from_none, from_far, *slots[near:])

    norms = mean_squares(plan, layout, keep, other, came[0])[:, :SLOTS].T
    norms = jnp.concatenate([norms] + [exchange(norms, "wide", k) for k in range(1, near)], axis=0)
    norms = jnp.concatenate([norms, exchange(norms, "wide", near)], axis=0)
    rows = plan[layout.norm : layout.norm + SLOTS]
    here = rows[:, None] == jnp.arange(norms.shape[0], dtype=jnp.int32)[None, :]
    ladder_norms = jnp.sum(jnp.where(here[:, :, None], norms[None], 0.0), axis=1)
    residual_out = add_at_home(plan, layout, cleared, held, [keep, other] + came)
    return (residual_out, ladder_norms)


def solution(mesh):
    in_specs = (P(None, ("wide", "narrow"), None), P(), P("wide", "narrow", None), P(), P(), P())
    out_specs = (P("wide", "narrow", None), P("wide", "narrow"))
    return jax.shard_map(body, mesh=mesh, in_specs=in_specs, out_specs=out_specs, check_vma=False)
```
